32 devices in a mesh: layer: 2 (over y), tok: 4 (over z), task: 4 (over x, core).
Axes of the slice: x: 2, y: 2, z: 4, core: 2. Of those that a mesh axis runs over, the one named last changes fastest.
Arguments:
- activations: bfloat16 [56, 56, 1024], P('tok', 'layer', 'task'), parts along dimension 1
- counts: int32 [56, 1024], P(('layer', 'tok'), 'task'), parts along dimension 0, may hold values from 28 to 56
- candidates: int32 [56, 2], P('layer'), parts along dimension 0, may hold values from 0 to 27, as said below
Outputs:
- correlation: bfloat16 [28, 4, 1024, 1024], P('tok', 'layer', 'task'), parts along dimension 1
The draws below stay inside these ranges and needn't reach their ends.
There are 2 independent parts, one for each index of `layer`. The reference program is written for one: setup_inputs(seed, part) draws one part's arguments, and reference() takes and returns one part's arrays. A program takes and returns all parts, laid end to end along the dimension named above; each array names one. Nothing has to cross between parts.
Inputs may be any that keep to these rules, and one draw needn't show every extreme that they name: `candidates`: row blocks b with equal b // 7 form one owner's 7 * 2 pairs; of their column blocks at most 4 have any one value of c // 7, and some value has exactly 4.
All inputs are finite; a program needn't handle non-finite values.
Results may differ from the reference program's by a relative error of at most 0.0057.
Values may be sent and summed in bfloat16 or wider, within the bound.
A program may use at most 64 MiB of HBM per device.

```python
import jax
import jax.numpy as jnp
from jax import lax

BLK = 1024
BPD = 7
CAND = 2
TOKENS = 56
BLOCKS = 28


def draw_activations(key, part):
    key = jax.random.fold_in(key, 5)
    keys = jax.random.split(key, 6)
    shape = (TOKENS, BLOCKS, BLK)
    signal = jax.random.normal(keys[0], (TOKENS, 1, BLK), jnp.float32)
    noise = jax.random.normal(keys[1], shape, jnp.float32)
    scale = jnp.exp(jax.random.uniform(keys[2], (1, BLOCKS, BLK), jnp.float32, jnp.log(0.3), jnp.log(4.0)))
    tok_scale = jnp.exp(jax.random.uniform(keys[5], (TOKENS, 1, 1), jnp.float32, jnp.log(0.7), jnp.log(2.0)))
    mixing = jax.random.uniform(keys[3], (1, BLOCKS, BLK), jnp.float32, -1.5, 1.5)
    offset = 2.0 * jax.random.normal(keys[4], (1, BLOCKS, BLK), jnp.float32)
    values = scale * (offset + tok_scale * (mixing * signal + noise))
    return values.astype(jnp.bfloat16)


def draw_candidates(key, part):
    key = jax.random.fold_in(key, 11)
    keys = jax.random.split(key, 3)
    owners = BLOCKS // BPD
    per_owner = BPD * CAND
    shifts = jax.random.randint(keys[0], (owners, 1), 0, owners)
    slot_ids = jnp.arange(per_owner, dtype=jnp.int32)[None, :]
    source = (jnp.arange(owners, dtype=jnp.int32)[:, None] + shifts + slot_ids) % owners
    within_block = jax.random.randint(keys[1], (owners, per_owner), 0, BPD)
    column = source * BPD + within_block
    column = jax.random.permutation(keys[2], column, axis=1, independent=True)
    return column.reshape(BLOCKS, CAND).astype(jnp.int32)


def with_ends(drawn, stream_key, low, top_value):
    index_at = [jax.random.randint(jax.random.fold_in(stream_key, axis), (), 0, length) for axis, length in enumerate(drawn.shape)]
    widest = drawn.shape.index(max(drawn.shape))
    next_to = index_at[:widest] + [(index_at[widest] + 1) % drawn.shape[widest]] + index_at[widest + 1:]
    return drawn.at[tuple(index_at)].set(low).at[tuple(next_to)].set(top_value)


def setup_inputs(seed: int = 0, part: int = 0) -> dict:
    key_of = jax.random.split(jax.random.key(seed), 4)
    part_splits = jax.random.split(jax.random.fold_in(key_of[3], part), 4)
    return {
        "activations": draw_activations(jax.random.fold_in(jax.random.fold_in(key_of[3], part), 71), part),
        "counts": with_ends(jax.random.randint(part_splits[1], (BLOCKS, BLK), TOKENS // 2, TOKENS + 1), jax.random.fold_in(part_splits[1], 1), TOKENS // 2, TOKENS).astype(jnp.int32),
        "candidates": draw_candidates(jax.random.fold_in(jax.random.fold_in(key_of[3], part), 71), part),
    }


def normalize(values, counts):
    token_ids = jnp.arange(values.shape[0], dtype=jnp.int32)[:, None, None]
    live_mask = (token_ids < counts[None]).astype(jnp.float32)
    count_f = counts.astype(jnp.float32)
    widened = values.astype(jnp.float32)
    unit_mean = lax.optimization_barrier(jnp.sum(widened * live_mask, axis=0)) / count_f
    centered = (widened - unit_mean) * live_mask
    variance = lax.optimization_barrier(jnp.sum(centered * centered, axis=0)) / count_f
    return (centered * lax.rsqrt(variance + 1e-05) * lax.rsqrt(count_f)).astype(jnp.bfloat16)

def reference(activations, counts, candidates):
    scaled = normalize(activations, counts)
    row_ids = jnp.repeat(jnp.arange(BLOCKS, dtype=jnp.int32), CAND)
    col_ids = candidates.reshape(-1).astype(jnp.int32)

    def pair_tile(pair_ids):
        row_part = lax.dynamic_index_in_dim(scaled, pair_ids[0], 1, keepdims=False)
        col_part = lax.dynamic_index_in_dim(scaled, pair_ids[1], 1, keepdims=False)
        return jnp.dot(row_part.T, col_part, preferred_element_type=jnp.float32).astype(jnp.bfloat16)
    tile_set = lax.map(pair_tile, (row_ids, col_ids))
    return tile_set.reshape(BLOCKS, CAND, BLK, BLK)
```

```python
import functools

import jax
import jax.numpy as jnp
from jax import lax
from jax.experimental import pallas as pl
from jax.experimental.pallas import tpu as pltpu
from jax.sharding import PartitionSpec as P

MESH = pl.DeviceIdType.MESH
ROWS = 16


def normalize(values, counts):
    token_ids = jnp.arange(values.shape[0], dtype=jnp.int32)[:, None, None]
    live_mask = (token_ids < counts[None]).astype(jnp.float32)
    count_f = counts.astype(jnp.float32)
    widened = values.astype(jnp.float32)
    unit_mean = jnp.sum(widened * live_mask, axis=0) / count_f
    centered = (widened - unit_mean) * live_mask
    variance = jnp.sum(centered * centered, axis=0) / count_f
    return (centered * lax.rsqrt(variance + 1e-05) * lax.rsqrt(count_f)).astype(jnp.bfloat16)


def body(activations, counts, candidates):
    tok_count = lax.axis_size("tok")
    task_count = lax.axis_size("task")
    owned_raw = lax.all_to_all(activations, "tok", split_axis=1, concat_axis=0, tiled=True)
    scaled = normalize(owned_raw, counts)
    blocks_per = scaled.shape[1]
    slice_width = scaled.shape[2]
    full_width = slice_width * task_count
    cand_count = candidates.shape[1]
    per_owner = blocks_per * cand_count
    capacity = (per_owner + tok_count - 1) // tok_count
    wanted = candidates.reshape(tok_count, per_owner)
    source = wanted // blocks_per
    within_block = wanted % blocks_per
    order_ids = jnp.arange(per_owner, dtype=jnp.int32)
    earlier = order_ids[None, :] < order_ids[:, None]
    same_source = source[:, :, None] == source[:, None, :]
    rank_in = jnp.sum((same_source & earlier[None]).astype(jnp.int32), axis=2)
    my_index = lax.axis_index("tok")
    slot_ids = jnp.arange(capacity, dtype=jnp.int32)
    matched = (
        (source == my_index)[:, :, None] & (rank_in[:, :, None] == slot_ids[None, None, :])
    ).astype(jnp.int32)
    picked = jnp.sum(matched * within_block[:, :, None], axis=1).reshape(-1)
    filled = jnp.sum(matched, axis=1).reshape(-1)
    send_buffer = jnp.where(
        (filled > 0)[None, :, None], jnp.take(scaled, picked, axis=1), jnp.zeros((), jnp.bfloat16)
    )
    received = lax.all_to_all(send_buffer, "tok", split_axis=1, concat_axis=1, tiled=True)
    my_source = lax.dynamic_index_in_dim(source, my_index, 0, keepdims=False)
    my_rank = lax.dynamic_index_in_dim(rank_in, my_index, 0, keepdims=False)
    columns = jnp.take(received, my_source * capacity + my_rank, axis=1)
    rows_pair = jnp.repeat(scaled, cand_count, axis=1)
    tile_set = jnp.einsum(
        "tps,tpc->psc",
        rows_pair,
        lax.all_gather(columns, "task", axis=2, tiled=True),
        preferred_element_type=jnp.float32,
    ).astype(jnp.bfloat16)
    return tile_set.reshape(blocks_per, cand_count, slice_width, full_width)


def flip(index, bit):
    return index + bit - 2 * bit * ((index // bit) % 2)


def exchange_kernel(tok_count, blocks_per, cand_count, act_ref, counts_ref, cand_ref, out_ref,
                    padded, count_rows, select, sending, z_send, z_recv, x_send, x_recv,
                    s_send, s_recv, r_send, r_recv):
    me = lax.axis_index("tok")
    task = lax.axis_index("task")
    partner = flip(task, 2)
    sibling = flip(task, 1)
    pairs = blocks_per * cand_count
    slots = pairs + blocks_per
    tokens, blocks, width = act_ref.shape
    rows, held = padded.shape[0], padded.shape[1]

    def tok_peer(k):
        other = me
        if k & 1:
            other = flip(other, 1)
        if k & 2:
            other = flip(other, 2)
        return other

    barrier = pltpu.get_barrier_semaphore()
    for k in range(1, tok_count):
        pl.semaphore_signal(barrier, inc=1, device_id={"tok": tok_peer(k)}, device_id_type=MESH)
    for other in (partner, sibling):
        pl.semaphore_signal(barrier, inc=1, device_id={"task": other}, device_id_type=MESH)

    padded[...] = jnp.zeros_like(padded)
    padded[0:tokens, 0:blocks, :] = act_ref[...]
    count_rows[...] = jnp.zeros_like(count_rows)
    counts = counts_ref[...]
    for owner in range(tok_count):
        mine = jnp.where(me == owner, counts, 0)
        at = pl.ds(owner * blocks_per, blocks_per)
        count_rows[0, at, :] = (mine // 16).astype(jnp.float32)
        count_rows[1, at, :] = (mine % 16).astype(jnp.float32)
    padded[tokens:tokens + 2] = count_rows[...].astype(jnp.bfloat16)
    flat = padded[...].reshape(rows * held, width)
    lane = lax.broadcasted_iota(jnp.int32, (rows, rows * held), 1)
    row = lax.broadcasted_iota(jnp.int32, (rows, rows * held), 0)
    offset = lane - held * row

    def pick(owner):
        for slot in range(slots):
            if slot < pairs:
                block = cand_ref[owner * blocks_per + slot // cand_count, slot % cand_count]
            else:
                block = owner * blocks_per + (slot - pairs)
            select[slot] = jnp.where(offset == block, 1.0, 0.0).astype(jnp.bfloat16)
        picked = jnp.dot(
            select[...].reshape(slots * rows, rows * held), flat, preferred_element_type=jnp.float32
        )
        return picked.astype(jnp.bfloat16).reshape(slots, rows, width)

    def z_copy(k):
        return pltpu.make_async_remote_copy(
            src_ref=sending.at[k], dst_ref=out_ref.at[task, me], send_sem=z_send.at[k],
            recv_sem=z_recv.at[k], device_id={"tok": tok_peer(k)}, device_id_type=MESH)

    def z_arrival(k):
        return pltpu.make_async_remote_copy(
            src_ref=sending.at[k], dst_ref=out_ref.at[task, tok_peer(k)], send_sem=z_send.at[k],
            recv_sem=z_recv.at[k], device_id={"tok": tok_peer(k)}, device_id_type=MESH)

    def task_copy(quarter, k, target, send, recv):
        view = out_ref.at[quarter, tok_peer(k), 0:pairs]
        return pltpu.make_async_remote_copy(
            src_ref=view, dst_ref=view, send_sem=send.at[k],
            recv_sem=recv.at[k], device_id={"task": target}, device_id_type=MESH)

    order = [k for k in (2, 3, 1) if k < tok_count]
    first = True
    for k in order:
        sending[k] = pick(tok_peer(k))
        if first:
            pl.semaphore_wait(barrier, tok_count + 1)
            first = False
        z_copy(k).start()
    out_ref[task, me] = pick(me)

    def pass_on(k):
        task_copy(task, k, partner, x_send, x_recv).start()
        task_copy(task, k, sibling, s_send, s_recv).start()

    def relay(k):
        task_copy(partner, k, partner, x_send, x_recv).wait_recv()
        task_copy(partner, k, sibling, r_send, r_recv).start()

    pass_on(0)
    before = 0
    for k in order:
        z_arrival(k).wait_recv()
        pass_on(k)
        relay(before)
        before = k
    relay(before)
    for k in range(tok_count):
        task_copy(sibling, k, sibling, s_send, s_recv).wait_recv()
        task_copy(flip(sibling, 2), k, sibling, r_send, r_recv).wait_recv()
        if k:
            z_copy(k).wait_send()
        task_copy(task, k, partner, x_send, x_recv).wait_send()
        task_copy(task, k, sibling, s_send, s_recv).wait_send()
        task_copy(partner, k, sibling, r_send, r_recv).wait_send()


def standardise(tiles, tokens):
    sources, rows, width = tiles.shape
    values = tiles.astype(jnp.float32)
    count_f = jnp.sum(values[:, tokens:tokens + 1] * 16.0 + values[:, tokens + 1:tokens + 2], axis=0)
    row = lax.broadcasted_iota(jnp.int32, (sources, rows, width), 1)
    source = lax.broadcasted_iota(jnp.int32, (sources, rows, width), 0)
    token = jnp.where(row < tokens, row + source * tokens, sources * rows).astype(jnp.float32)
    live = token < count_f[None]
    kept = jnp.where(live, values, 0.0)
    mean = jnp.sum(jnp.sum(kept, axis=0), axis=0, keepdims=True) / count_f
    centered = jnp.where(live, values - mean[None], 0.0)
    variance = jnp.sum(jnp.sum(centered * centered, axis=0), axis=0, keepdims=True) / count_f
    scaled = centered * lax.rsqrt(variance + 1e-05)[None] * lax.rsqrt(count_f)[None]
    return scaled.astype(jnp.bfloat16).reshape(sources * rows, width)


def tile_kernel(tokens, cand_count, buf_ref, out_ref):
    task_count = buf_ref.shape[0]
    width = buf_ref.shape[4]
    step = pl.program_id(0)
    pairs = cand_count * pl.num_programs(0)
    task = lax.axis_index("task")
    left = standardise(buf_ref[task, :, pairs + step], tokens)
    for cand in range(cand_count):
        for quarter in range(task_count):
            right = standardise(buf_ref[quarter, :, cand_count * step + cand], tokens)
            tile = lax.dot_general(left, right, (((0,), (0,)), ((), ())), preferred_element_type=jnp.float32)
            out_ref[0, cand, :, quarter * width:(quarter + 1) * width] = tile.astype(jnp.bfloat16)


def kernel_body(activations, counts, candidates):
    tok_count = lax.axis_size("tok")
    task_count = lax.axis_size("task")
    tokens, blocks, width = activations.shape
    blocks_per = counts.shape[0]
    cand_count = candidates.shape[1]
    pairs = blocks_per * cand_count
    slots = pairs + blocks_per
    held = (blocks + 15) // 16 * 16
    tile = (slots, ROWS, width)
    gathered = pl.pallas_call(
        functools.partial(exchange_kernel, tok_count, blocks_per, cand_count),
        out_shape=jax.ShapeDtypeStruct((task_count, tok_count) + tile, jnp.bfloat16),
        in_specs=[
            pl.BlockSpec(memory_space=pltpu.VMEM),
            pl.BlockSpec(memory_space=pltpu.VMEM),
            pl.BlockSpec(memory_space=pltpu.SMEM),
        ],
        out_specs=pl.BlockSpec(memory_space=pltpu.VMEM),
        scratch_shapes=[
            pltpu.VMEM((ROWS, held, width), jnp.bfloat16),
            pltpu.VMEM((2, held, width), jnp.float32),
            pltpu.VMEM((slots, ROWS, ROWS * held), jnp.bfloat16),
            pltpu.VMEM((tok_count,) + tile, jnp.bfloat16),
        ] + [pltpu.SemaphoreType.DMA((tok_count,))] * 8,
        compiler_params=pltpu.CompilerParams(
            collective_id=0, has_side_effects=True, vmem_limit_bytes=32 * 2**20
        ),
        name="exchange",
    )(activations, counts, candidates)
    return pl.pallas_call(
        functools.partial(tile_kernel, tokens, cand_count),
        grid=(blocks_per,),
        out_shape=jax.ShapeDtypeStruct((blocks_per, cand_count, width, width * task_count), jnp.bfloat16),
        in_specs=[pl.BlockSpec(memory_space=pltpu.VMEM)],
        out_specs=pl.BlockSpec((1, cand_count, width, width * task_count), lambda i: (i, 0, 0, 0)),
        compiler_params=pltpu.CompilerParams(vmem_limit_bytes=32 * 2**20),
        name="tiles",
    )(gathered)


def solution(mesh):
    small = mesh.shape["tok"] == 4 and mesh.shape["task"] == 4
    return jax.shard_map(
        kernel_body if small else body,
        mesh=mesh,
        in_specs=(P("tok", "layer", "task"), P(("layer", "tok"), "task"), P("layer", None)),
        out_specs=P("tok", "layer", "task", None),
        check_vma=False,
    )
```

```python
import functools

import jax
import jax.numpy as jnp
from jax import lax
from jax.experimental import pallas as pl
from jax.experimental.pallas import tpu as pltpu
from jax.sharding import PartitionSpec as P

MESH = pl.DeviceIdType.MESH
ROWS = 16
CHUNK = 7
ORDER = (2, 3, 1)


def normalize(values, counts):
    token_ids = jnp.arange(values.shape[0], dtype=jnp.int32)[:, None, None]
    live_mask = (token_ids < counts[None]).astype(jnp.float32)
    count_f = counts.astype(jnp.float32)
    widened = values.astype(jnp.float32)
    unit_mean = jnp.sum(widened * live_mask, axis=0) / count_f
    centered = (widened - unit_mean) * live_mask
    variance = jnp.sum(centered * centered, axis=0) / count_f
    return (centered * lax.rsqrt(variance + 1e-05) * lax.rsqrt(count_f)).astype(jnp.bfloat16)


def body(activations, counts, candidates):
    tok_count = lax.axis_size("tok")
    task_count = lax.axis_size("task")
    owned_raw = lax.all_to_all(activations, "tok", split_axis=1, concat_axis=0, tiled=True)
    scaled = normalize(owned_raw, counts)
    blocks_per = scaled.shape[1]
    slice_width = scaled.shape[2]
    full_width = slice_width * task_count
    cand_count = candidates.shape[1]
    per_owner = blocks_per * cand_count
    capacity = (per_owner + tok_count - 1) // tok_count
    wanted = candidates.reshape(tok_count, per_owner)
    source = wanted // blocks_per
    within_block = wanted % blocks_per
    order_ids = jnp.arange(per_owner, dtype=jnp.int32)
    earlier = order_ids[None, :] < order_ids[:, None]
    same_source = source[:, :, None] == source[:, None, :]
    rank_in = jnp.sum((same_source & earlier[None]).astype(jnp.int32), axis=2)
    my_index = lax.axis_index("tok")
    slot_ids = jnp.arange(capacity, dtype=jnp.int32)
    matched = (
        (source == my_index)[:, :, None] & (rank_in[:, :, None] == slot_ids[None, None, :])
    ).astype(jnp.int32)
    picked = jnp.sum(matched * within_block[:, :, None], axis=1).reshape(-1)
    filled = jnp.sum(matched, axis=1).reshape(-1)
    send_buffer = jnp.where(
        (filled > 0)[None, :, None], jnp.take(scaled, picked, axis=1), jnp.zeros((), jnp.bfloat16)
    )
    received = lax.all_to_all(send_buffer, "tok", split_axis=1, concat_axis=1, tiled=True)
    my_source = lax.dynamic_index_in_dim(source, my_index, 0, keepdims=False)
    my_rank = lax.dynamic_index_in_dim(rank_in, my_index, 0, keepdims=False)
    columns = jnp.take(received, my_source * capacity + my_rank, axis=1)
    rows_pair = jnp.repeat(scaled, cand_count, axis=1)
    tile_set = jnp.einsum(
        "tps,tpc->psc",
        rows_pair,
        lax.all_gather(columns, "task", axis=2, tiled=True),
        preferred_element_type=jnp.float32,
    ).astype(jnp.bfloat16)
    return tile_set.reshape(blocks_per, cand_count, slice_width, full_width)


def flip(index, bit):
    return index + bit - 2 * bit * ((index // bit) % 2)


def exchange_kernel(tok_count, blocks_per, cand_count, act_hbm, counts_hbm, cand_ref, out_ref,
                    act_ref, counts_ref, local, padded, count_rows, select, sending, z_send, z_recv, x_send, x_recv,
                    s_send, s_recv, r_send, r_recv):
    me = lax.axis_index("tok")
    task = lax.axis_index("task")
    partner = flip(task, 2)
    sibling = flip(task, 1)
    pairs = blocks_per * cand_count
    slots = pairs + blocks_per
    tokens, blocks, width = act_ref.shape
    reads = [pltpu.make_async_copy(act_hbm, act_ref, local.at[0]), pltpu.make_async_copy(counts_hbm, counts_ref, local.at[1])]
    for read in reads:
        read.start()
    rows, held = padded.shape[0], padded.shape[1]

    def tok_peer(k):
        other = me
        if k & 1:
            other = flip(other, 1)
        if k & 2:
            other = flip(other, 2)
        return other

    barrier = pltpu.get_barrier_semaphore()
    for k in range(1, tok_count):
        pl.semaphore_signal(barrier, inc=1, device_id={"tok": tok_peer(k)}, device_id_type=MESH)
    for other in (partner, sibling):
        pl.semaphore_signal(barrier, inc=1, device_id={"task": other}, device_id_type=MESH)

    padded[...] = jnp.zeros_like(padded)
    count_rows[...] = jnp.zeros_like(count_rows)
    for read in reads:
        read.wait()
    padded[0:tokens, 0:blocks, :] = act_ref[...]
    counts = counts_ref[...]
    for owner in range(tok_count):
        mine = jnp.where(me == owner, counts, 0)
        at = pl.ds(owner * blocks_per, blocks_per)
        count_rows[0, at, :] = (mine // 16).astype(jnp.float32)
        count_rows[1, at, :] = (mine % 16).astype(jnp.float32)
    padded[tokens:tokens + 2] = count_rows[...].astype(jnp.bfloat16)
    flat = padded[...].reshape(rows * held, width)
    lane = lax.broadcasted_iota(jnp.int32, (rows, rows * held), 1)
    row = lax.broadcasted_iota(jnp.int32, (rows, rows * held), 0)
    offset = lane - held * row

    def pick(owner):
        for slot in range(slots):
            if slot < pairs:
                block = cand_ref[slot % cand_count, owner * blocks_per + slot // cand_count]
            else:
                block = owner * blocks_per + (slot - pairs)
            select[slot] = jnp.where(offset == block, 1.0, 0.0).astype(jnp.bfloat16)
        picked = jnp.dot(
            select[...].reshape(slots * rows, rows * held), flat, preferred_element_type=jnp.float32
        )
        return picked.astype(jnp.bfloat16).reshape(slots, rows, width)

    chunks = [(lo, min(lo + CHUNK, pairs)) for lo in range(0, pairs, CHUNK)] + [(pairs, slots)]
    passed = range(len(chunks) - 1)

    def z_copy(k, c, source=None):
        lo, hi = chunks[c]
        return pltpu.make_async_remote_copy(
            src_ref=sending.at[k, lo:hi], dst_ref=out_ref.at[task, me if source is None else source, lo:hi],
            send_sem=z_send.at[k, c], recv_sem=z_recv.at[k, c],
            device_id={"tok": tok_peer(k)}, device_id_type=MESH)

    def task_copy(quarter, k, c, target, send, recv):
        lo, hi = chunks[c]
        view = out_ref.at[quarter, tok_peer(k), lo:hi]
        return pltpu.make_async_remote_copy(
            src_ref=view, dst_ref=view, send_sem=send.at[k, c],
            recv_sem=recv.at[k, c], device_id={"task": target}, device_id_type=MESH)

    def pass_on(k, c):
        task_copy(task, k, c, partner, x_send, x_recv).start()
        task_copy(task, k, c, sibling, s_send, s_recv).start()

    def relay(k, c):
        task_copy(partner, k, c, partner, x_send, x_recv).wait_recv()
        task_copy(partner, k, c, sibling, r_send, r_recv).start()

    order = [k for k in ORDER if k < tok_count]
    for k in order:
        sending[k] = pick(tok_peer(k))
    out_ref[task, me] = pick(me)
    pl.semaphore_wait(barrier, tok_count + 1)
    for c in range(len(chunks)):
        for k in order:
            z_copy(k, c).start()
        if c == 0:
            for own in passed:
                pass_on(0, own)
    waiting = [(0, c) for c in passed]
    for c in passed:
        for k in order:
            z_copy(k, c, tok_peer(k)).wait_recv()
            pass_on(k, c)
            waiting.append((k, c))
            relay(*waiting.pop(0))
    for k, c in waiting:
        relay(k, c)
    for k in order:
        z_copy(k, len(chunks) - 1, tok_peer(k)).wait_recv()
        for c in range(len(chunks)):
            z_copy(k, c).wait_send()
    for k in range(tok_count):
        for c in passed:
            task_copy(sibling, k, c, sibling, s_send, s_recv).wait_recv()
            task_copy(flip(sibling, 2), k, c, sibling, r_send, r_recv).wait_recv()
            task_copy(task, k, c, partner, x_send, x_recv).wait_send()
            task_copy(task, k, c, sibling, s_send, s_recv).wait_send()
            task_copy(partner, k, c, sibling, r_send, r_recv).wait_send()


def standardise(tiles, tokens):
    sources, rows, width = tiles.shape
    values = tiles.astype(jnp.float32)
    count_f = jnp.sum(values[:, tokens:tokens + 1] * 16.0 + values[:, tokens + 1:tokens + 2], axis=0)
    row = lax.broadcasted_iota(jnp.int32, (sources, rows, width), 1)
    source = lax.broadcasted_iota(jnp.int32, (sources, rows, width), 0)
    token = jnp.where(row < tokens, row + source * tokens, sources * rows).astype(jnp.float32)
    live = token < count_f[None]
    kept = jnp.where(live, values, 0.0)
    mean = jnp.sum(jnp.sum(kept, axis=0), axis=0, keepdims=True) / count_f
    centered = jnp.where(live, values - mean[None], 0.0)
    variance = jnp.sum(jnp.sum(centered * centered, axis=0), axis=0, keepdims=True) / count_f
    scaled = centered * (lax.rsqrt(variance + 1e-05) * lax.rsqrt(count_f))[None]
    return scaled.astype(jnp.bfloat16).reshape(sources * rows, width)


def tile_kernel(tokens, cand_count, buf_ref, out_ref):
    task_count = buf_ref.shape[0]
    width = buf_ref.shape[4]
    step = pl.program_id(0)
    pairs = cand_count * pl.num_programs(0)
    task = lax.axis_index("task")
    left = standardise(buf_ref[task, :, pairs + step], tokens)
    for cand in range(cand_count):
        for quarter in range(task_count):
            right = standardise(buf_ref[quarter, :, cand_count * step + cand], tokens)
            tile = lax.dot_general(left, right, (((0,), (0,)), ((), ())), preferred_element_type=jnp.float32)
            out_ref[0, cand, :, quarter * width:(quarter + 1) * width] = tile.astype(jnp.bfloat16)


def kernel_body(activations, counts, candidates):
    tok_count = lax.axis_size("tok")
    task_count = lax.axis_size("task")
    tokens, blocks, width = activations.shape
    blocks_per = counts.shape[0]
    cand_count = candidates.shape[1]
    pairs = blocks_per * cand_count
    slots = pairs + blocks_per
    held = (blocks + 15) // 16 * 16
    tile = (slots, ROWS, width)
    gathered = pl.pallas_call(
        functools.partial(exchange_kernel, tok_count, blocks_per, cand_count),
        out_shape=jax.ShapeDtypeStruct((task_count, tok_count) + tile, jnp.bfloat16),
        in_specs=[
            pl.BlockSpec(memory_space=pltpu.HBM),
            pl.BlockSpec(memory_space=pltpu.HBM),
            pl.BlockSpec(memory_space=pltpu.SMEM),
        ],
        out_specs=pl.BlockSpec(memory_space=pltpu.VMEM),
        scratch_shapes=[
            pltpu.VMEM(activations.shape, jnp.bfloat16),
            pltpu.VMEM(counts.shape, jnp.int32),
            pltpu.SemaphoreType.DMA((2,)),
            pltpu.VMEM((ROWS, held, width), jnp.bfloat16),
            pltpu.VMEM((2, held, width), jnp.float32),
            pltpu.VMEM((slots, ROWS, ROWS * held), jnp.bfloat16),
            pltpu.VMEM((tok_count,) + tile, jnp.bfloat16),
        ] + [pltpu.SemaphoreType.DMA((tok_count, pairs // CHUNK + 2))] * 8,
        compiler_params=pltpu.CompilerParams(
            collective_id=0, has_side_effects=True, vmem_limit_bytes=32 * 2**20
        ),
        name="exchange",
    )(*[pltpu.with_memory_space_constraint(x, pltpu.HBM) for x in (activations, counts)], candidates.T)
    return pl.pallas_call(
        functools.partial(tile_kernel, tokens, cand_count),
        grid=(blocks_per,),
        out_shape=jax.ShapeDtypeStruct((blocks_per, cand_count, width, width * task_count), jnp.bfloat16),
        in_specs=[pl.BlockSpec(memory_space=pltpu.VMEM)],
        out_specs=pl.BlockSpec((1, cand_count, width, width * task_count), lambda i: (i, 0, 0, 0)),
        compiler_params=pltpu.CompilerParams(vmem_limit_bytes=32 * 2**20),
        name="tiles",
    )(gathered)


def solution(mesh):
    small = mesh.shape["tok"] == 4 and mesh.shape["task"] == 4
    return jax.shard_map(
        kernel_body if small else body,
        mesh=mesh,
        in_specs=(P("tok", "layer", "task"), P(("layer", "tok"), "task"), P("layer", None)),
        out_specs=P("tok", "layer", "task", None),
        check_vma=False,
    )
```

```python
import functools

import jax
import jax.numpy as jnp
from jax import lax
from jax.experimental import pallas as pl
from jax.experimental.pallas import tpu as pltpu
from jax.sharding import PartitionSpec as P

MESH = pl.DeviceIdType.MESH
ROWS = 16
CHUNK = 4
AHEAD = 2
LAG = 1
ORDER = (1, 2, 3)


def normalize(values, counts):
    token_ids = jnp.arange(values.shape[0], dtype=jnp.int32)[:, None, None]
    live_mask = (token_ids < counts[None]).astype(jnp.float32)
    count_f = counts.astype(jnp.float32)
    widened = values.astype(jnp.float32)
    unit_mean = jnp.sum(widened * live_mask, axis=0) / count_f
    centered = (widened - unit_mean) * live_mask
    variance = jnp.sum(centered * centered, axis=0) / count_f
    return (centered * lax.rsqrt(variance + 1e-05) * lax.rsqrt(count_f)).astype(jnp.bfloat16)


def body(activations, counts, candidates):
    tok_count = lax.axis_size("tok")
    task_count = lax.axis_size("task")
    owned_raw = lax.all_to_all(activations, "tok", split_axis=1, concat_axis=0, tiled=True)
    scaled = normalize(owned_raw, counts)
    blocks_per = scaled.shape[1]
    slice_width = scaled.shape[2]
    full_width = slice_width * task_count
    cand_count = candidates.shape[1]
    per_owner = blocks_per * cand_count
    capacity = (per_owner + tok_count - 1) // tok_count
    wanted = candidates.reshape(tok_count, per_owner)
    source = wanted // blocks_per
    within_block = wanted % blocks_per
    order_ids = jnp.arange(per_owner, dtype=jnp.int32)
    earlier = order_ids[None, :] < order_ids[:, None]
    same_source = source[:, :, None] == source[:, None, :]
    rank_in = jnp.sum((same_source & earlier[None]).astype(jnp.int32), axis=2)
    my_index = lax.axis_index("tok")
    slot_ids = jnp.arange(capacity, dtype=jnp.int32)
    matched = (
        (source == my_index)[:, :, None] & (rank_in[:, :, None] == slot_ids[None, None, :])
    ).astype(jnp.int32)
    picked = jnp.sum(matched * within_block[:, :, None], axis=1).reshape(-1)
    filled = jnp.sum(matched, axis=1).reshape(-1)
    send_buffer = jnp.where(
        (filled > 0)[None, :, None], jnp.take(scaled, picked, axis=1), jnp.zeros((), jnp.bfloat16)
    )
    received = lax.all_to_all(send_buffer, "tok", split_axis=1, concat_axis=1, tiled=True)
    my_source = lax.dynamic_index_in_dim(source, my_index, 0, keepdims=False)
    my_rank = lax.dynamic_index_in_dim(rank_in, my_index, 0, keepdims=False)
    columns = jnp.take(received, my_source * capacity + my_rank, axis=1)
    rows_pair = jnp.repeat(scaled, cand_count, axis=1)
    tile_set = jnp.einsum(
        "tps,tpc->psc",
        rows_pair,
        lax.all_gather(columns, "task", axis=2, tiled=True),
        preferred_element_type=jnp.float32,
    ).astype(jnp.bfloat16)
    return tile_set.reshape(blocks_per, cand_count, slice_width, full_width)


def flip(index, bit):
    return index + bit - 2 * bit * ((index // bit) % 2)


def exchange_kernel(tok_count, blocks_per, cand_count, act_hbm, counts_hbm, cand_hbm, cols_ref, rows_ref,
                    out_ref, act_ref, counts_ref, cand_ref, local, padded, count_rows, select, sending, z_send, z_recv, x_send, x_recv,
                    s_send, s_recv, r_send, r_recv):
    me = lax.axis_index("tok")
    task = lax.axis_index("task")
    partner = flip(task, 2)
    sibling = flip(task, 1)
    pairs = blocks_per * cand_count
    slots = pairs + blocks_per
    tokens, blocks, width = act_ref.shape
    reads = [pltpu.make_async_copy(act_hbm, act_ref, local.at[0]), pltpu.make_async_copy(counts_hbm, counts_ref, local.at[1]),
             pltpu.make_async_copy(cand_hbm, cand_ref, local.at[2])]
    for read in reads:
        read.start()
    rows, held = padded.shape[0], padded.shape[1]

    def tok_peer(k):
        other = me
        if k & 1:
            other = flip(other, 1)
        if k & 2:
            other = flip(other, 2)
        return other

    barrier = pltpu.get_barrier_semaphore()
    for k in range(1, tok_count):
        pl.semaphore_signal(barrier, inc=1, device_id={"tok": tok_peer(k)}, device_id_type=MESH)
    for other in (partner, sibling):
        pl.semaphore_signal(barrier, inc=1, device_id={"task": other}, device_id_type=MESH)

    padded[...] = jnp.zeros_like(padded)
    count_rows[...] = jnp.zeros_like(count_rows)
    for read in reads:
        read.wait()
    padded[0:tokens, 0:blocks, :] = act_ref[...]
    counts = counts_ref[...]
    for owner in range(tok_count):
        mine = jnp.where(me == owner, counts, 0)
        at = pl.ds(owner * blocks_per, blocks_per)
        count_rows[0, at, :] = (mine // 16).astype(jnp.float32)
        count_rows[1, at, :] = (mine % 16).astype(jnp.float32)
    padded[tokens:tokens + 2] = count_rows[...].astype(jnp.bfloat16)
    flat = padded[...].reshape(rows * held, width)
    lane = lax.broadcasted_iota(jnp.int32, (rows, rows * held), 1)
    row = lax.broadcasted_iota(jnp.int32, (rows, rows * held), 0)
    offset = lane - held * row

    def pick(owner):
        for slot in range(slots):
            if slot < pairs:
                block = cand_ref[slot % cand_count, owner * blocks_per + slot // cand_count]
            else:
                block = owner * blocks_per + (slot - pairs)
            select[slot] = jnp.where(offset == block, 1.0, 0.0).astype(jnp.bfloat16)
        picked = jnp.dot(
            select[...].reshape(slots * rows, rows * held), flat, preferred_element_type=jnp.float32
        )
        return picked.astype(jnp.bfloat16).reshape(slots, rows, width)

    chunks = [(lo, min(lo + CHUNK, pairs)) for lo in range(0, pairs, CHUNK)] + [(pairs, slots)]
    passed = range(len(chunks) - 1)

    def z_copy(k, c, source=None):
        lo, hi = chunks[c]
        return pltpu.make_async_remote_copy(
            src_ref=sending.at[k, lo:hi], dst_ref=out_ref.at[task, me if source is None else source, lo:hi],
            send_sem=z_send.at[k, c], recv_sem=z_recv.at[k, c],
            device_id={"tok": tok_peer(k)}, device_id_type=MESH)

    def task_copy(quarter, k, c, target, send, recv):
        lo, hi = chunks[c]
        view = out_ref.at[quarter, tok_peer(k), lo:hi]
        return pltpu.make_async_remote_copy(
            src_ref=view, dst_ref=view, send_sem=send.at[k, c],
            recv_sem=recv.at[k, c], device_id={"task": target}, device_id_type=MESH)

    def pass_on(k, c):
        task_copy(task, k, c, partner, x_send, x_recv).start()
        task_copy(task, k, c, sibling, s_send, s_recv).start()

    def relay(k, c):
        task_copy(partner, k, c, partner, x_send, x_recv).wait_recv()
        task_copy(partner, k, c, sibling, r_send, r_recv).start()

    order = [k for k in ORDER if k < tok_count]
    for k in order:
        sending[k] = pick(tok_peer(k))
    out_ref[task, me] = pick(me)
    pl.semaphore_wait(barrier, tok_count + 1)
    for k in order:
        z_copy(k, 0).start()
    for own in passed:
        pass_on(0, own)
    for k in order:
        z_copy(k, 1).start()
    def finish(c):
        for k in range(tok_count):
            task_copy(sibling, k, c, sibling, s_send, s_recv).wait_recv()
            task_copy(flip(sibling, 2), k, c, sibling, r_send, r_recv).wait_recv()

        def one(slot, carry):
            for quarter in range(out_ref.shape[0]):
                cols_ref[slot, :, quarter * width:(quarter + 1) * width] = standardise(
                    out_ref[quarter, :, slot], tokens)
            return carry

        lax.fori_loop(chunks[c][0], chunks[c][1], one, 0)

    last = len(chunks) - 1
    waiting = [(0, c) for c in passed]
    for c in passed:
        for k in order:
            z_copy(k, c, tok_peer(k)).wait_recv()
            if c + AHEAD <= last:
                z_copy(k, c + AHEAD).start()
            pass_on(k, c)
            waiting.append((k, c))
            relay(*waiting.pop(0))
        if c >= LAG:
            for at in [at for at in waiting if at[1] <= c - LAG]:
                relay(*at)
                waiting.remove(at)
            finish(c - LAG)
    for k in order:
        z_copy(k, last, tok_peer(k)).wait_recv()
    for k, c in waiting:
        relay(k, c)

    def one_row(slot, carry):
        rows = standardise(out_ref[task, :, pairs + slot], tokens)
        rows_ref[slot] = rows.astype(jnp.float32).T.astype(jnp.bfloat16)
        return carry

    lax.fori_loop(0, blocks_per, one_row, 0)
    for c in range(max(len(passed) - LAG, 0), len(passed)):
        finish(c)
    for k in range(tok_count):
        if k:
            for c in range(len(chunks)):
                z_copy(k, c).wait_send()
        for c in passed:
            task_copy(task, k, c, partner, x_send, x_recv).wait_send()
            task_copy(task, k, c, sibling, s_send, s_recv).wait_send()
            task_copy(partner, k, c, sibling, r_send, r_recv).wait_send()


def standardise(tiles, tokens):
    sources, rows, width = tiles.shape
    values = tiles.astype(jnp.float32)
    count_f = jnp.sum(values[:, tokens:tokens + 1] * 16.0 + values[:, tokens + 1:tokens + 2], axis=0)
    row = lax.broadcasted_iota(jnp.int32, (sources, rows, width), 1)
    source = lax.broadcasted_iota(jnp.int32, (sources, rows, width), 0)
    token = jnp.where(row < tokens, row + source * tokens, sources * rows).astype(jnp.float32)
    live = token < count_f[None]
    kept = jnp.where(live, values, 0.0)
    mean = jnp.sum(jnp.sum(kept, axis=0), axis=0, keepdims=True) / count_f
    centered = jnp.where(live, values - mean[None], 0.0)
    variance = jnp.sum(jnp.sum(centered * centered, axis=0), axis=0, keepdims=True) / count_f
    scaled = centered * (lax.rsqrt(variance + 1e-05) * lax.rsqrt(count_f))[None]
    return scaled.astype(jnp.bfloat16).reshape(sources * rows, width)


def tile_kernel(cols_ref, rows_ref, out_ref, held, sems):
    step = pl.program_id(0)
    blocks_per, cand_count = held.shape[0], held.shape[1]
    left = rows_ref[step]
    for cand in range(cand_count):
        tile = jnp.dot(left, cols_ref[cand_count * step + cand], preferred_element_type=jnp.float32)
        held[step, cand] = tile.astype(jnp.bfloat16)
        pltpu.make_async_copy(held.at[step, cand], out_ref.at[step, cand], sems.at[step, cand]).start()

    @pl.when(step == blocks_per - 1)
    def _():
        for block in range(blocks_per):
            for cand in range(cand_count):
                pltpu.make_async_copy(held.at[block, cand], out_ref.at[block, cand], sems.at[block, cand]).wait()


def kernel_body(activations, counts, candidates):
    tok_count = lax.axis_size("tok")
    task_count = lax.axis_size("task")
    tokens, blocks, width = activations.shape
    blocks_per = counts.shape[0]
    cand_count = candidates.shape[1]
    pairs = blocks_per * cand_count
    slots = pairs + blocks_per
    held = (blocks + 15) // 16 * 16
    tile = (slots, ROWS, width)
    columns, rows = pl.pallas_call(
        functools.partial(exchange_kernel, tok_count, blocks_per, cand_count),
        out_shape=(
            jax.ShapeDtypeStruct((pairs, tok_count * ROWS, task_count * width), jnp.bfloat16),
            jax.ShapeDtypeStruct((blocks_per, width, tok_count * ROWS), jnp.bfloat16),
        ),
        in_specs=[
            pl.BlockSpec(memory_space=pltpu.HBM),
            pl.BlockSpec(memory_space=pltpu.HBM),
            pl.BlockSpec(memory_space=pltpu.HBM),
        ],
        out_specs=(pl.BlockSpec(memory_space=pltpu.VMEM),) * 2,
        scratch_shapes=[
            pltpu.VMEM((task_count, tok_count) + tile, jnp.bfloat16),
            pltpu.VMEM(activations.shape, jnp.bfloat16),
            pltpu.VMEM(counts.shape, jnp.int32),
            pltpu.SMEM(candidates.shape[::-1], jnp.int32),
            pltpu.SemaphoreType.DMA((3,)),
            pltpu.VMEM((ROWS, held, width), jnp.bfloat16),
            pltpu.VMEM((2, held, width), jnp.float32),
            pltpu.VMEM((slots, ROWS, ROWS * held), jnp.bfloat16),
            pltpu.VMEM((tok_count,) + tile, jnp.bfloat16),
        ] + [pltpu.SemaphoreType.DMA((tok_count, pairs // CHUNK + 2))] * 8,
        compiler_params=pltpu.CompilerParams(
            collective_id=0, has_side_effects=True, vmem_limit_bytes=32 * 2**20
        ),
        name="exchange",
    )(*[pltpu.with_memory_space_constraint(x, pltpu.HBM) for x in (activations, counts, candidates.T)])
    return pl.pallas_call(
        tile_kernel,
        grid=(blocks_per,),
        out_shape=jax.ShapeDtypeStruct((blocks_per, cand_count, width, width * task_count), jnp.bfloat16),
        in_specs=[pl.BlockSpec(memory_space=pltpu.VMEM)] * 2,
        out_specs=pl.BlockSpec(memory_space=pltpu.HBM),
        scratch_shapes=[
            pltpu.VMEM((blocks_per, cand_count, width, width * task_count), jnp.bfloat16),
            pltpu.SemaphoreType.DMA((blocks_per, cand_count)),
        ],
        compiler_params=pltpu.CompilerParams(vmem_limit_bytes=32 * 2**20),
        name="tiles",
    )(columns, rows)


def solution(mesh):
    small = mesh.shape["tok"] == 4 and mesh.shape["task"] == 4
    return jax.shard_map(
        kernel_body if small else body,
        mesh=mesh,
        in_specs=(P("tok", "layer", "task"), P(("layer", "tok"), "task"), P("layer", None)),
        out_specs=P("tok", "layer", "task", None),
        check_vma=False,
    )
```

```python
import functools

import jax
import jax.numpy as jnp
from jax import lax
from jax.experimental import pallas as pl
from jax.experimental.pallas import tpu as pltpu
from jax.sharding import PartitionSpec as P

MESH = pl.DeviceIdType.MESH
ROWS = 16
CHUNK = 7
AHEAD = 2
LAG = 1
ORDER = (1, 2, 3)


def normalize(values, counts):
    token_ids = jnp.arange(values.shape[0], dtype=jnp.int32)[:, None, None]
    live_mask = (token_ids < counts[None]).astype(jnp.float32)
    count_f = counts.astype(jnp.float32)
    widened = values.astype(jnp.float32)
    unit_mean = jnp.sum(widened * live_mask, axis=0) / count_f
    centered = (widened - unit_mean) * live_mask
    variance = jnp.sum(centered * centered, axis=0) / count_f
    return (centered * lax.rsqrt(variance + 1e-05) * lax.rsqrt(count_f)).astype(jnp.bfloat16)


def body(activations, counts, candidates):
    tok_count = lax.axis_size("tok")
    task_count = lax.axis_size("task")
    owned_raw = lax.all_to_all(activations, "tok", split_axis=1, concat_axis=0, tiled=True)
    scaled = normalize(owned_raw, counts)
    blocks_per = scaled.shape[1]
    slice_width = scaled.shape[2]
    full_width = slice_width * task_count
    cand_count = candidates.shape[1]
    per_owner = blocks_per * cand_count
    capacity = (per_owner + tok_count - 1) // tok_count
    wanted = candidates.reshape(tok_count, per_owner)
    source = wanted // blocks_per
    within_block = wanted % blocks_per
    order_ids = jnp.arange(per_owner, dtype=jnp.int32)
    earlier = order_ids[None, :] < order_ids[:, None]
    same_source = source[:, :, None] == source[:, None, :]
    rank_in = jnp.sum((same_source & earlier[None]).astype(jnp.int32), axis=2)
    my_index = lax.axis_index("tok")
    slot_ids = jnp.arange(capacity, dtype=jnp.int32)
    matched = (
        (source == my_index)[:, :, None] & (rank_in[:, :, None] == slot_ids[None, None, :])
    ).astype(jnp.int32)
    picked = jnp.sum(matched * within_block[:, :, None], axis=1).reshape(-1)
    filled = jnp.sum(matched, axis=1).reshape(-1)
    send_buffer = jnp.where(
        (filled > 0)[None, :, None], jnp.take(scaled, picked, axis=1), jnp.zeros((), jnp.bfloat16)
    )
    received = lax.all_to_all(send_buffer, "tok", split_axis=1, concat_axis=1, tiled=True)
    my_source = lax.dynamic_index_in_dim(source, my_index, 0, keepdims=False)
    my_rank = lax.dynamic_index_in_dim(rank_in, my_index, 0, keepdims=False)
    columns = jnp.take(received, my_source * capacity + my_rank, axis=1)
    rows_pair = jnp.repeat(scaled, cand_count, axis=1)
    tile_set = jnp.einsum(
        "tps,tpc->psc",
        rows_pair,
        lax.all_gather(columns, "task", axis=2, tiled=True),
        preferred_element_type=jnp.float32,
    ).astype(jnp.bfloat16)
    return tile_set.reshape(blocks_per, cand_count, slice_width, full_width)


def flip(index, bit):
    return index + bit - 2 * bit * ((index // bit) % 2)


def exchange_kernel(tok_count, blocks_per, cand_count, act_hbm, counts_hbm, cand_hbm, cols_ref, rows_ref,
                    out_ref, act_ref, counts_ref, cand_ref, local, padded, count_rows, select, sending, z_send, z_recv, x_send, x_recv,
                    s_send, s_recv, r_send, r_recv):
    me = lax.axis_index("tok")
    task = lax.axis_index("task")
    partner = flip(task, 2)
    sibling = flip(task, 1)
    pairs = blocks_per * cand_count
    slots = pairs + blocks_per
    tokens, blocks, width = act_ref.shape
    reads = [pltpu.make_async_copy(act_hbm, act_ref, local.at[0]), pltpu.make_async_copy(counts_hbm, counts_ref, local.at[1]),
             pltpu.make_async_copy(cand_hbm, cand_ref, local.at[2])]
    for read in reads:
        read.start()
    rows, held = padded.shape[0], padded.shape[1]

    def tok_peer(k):
        other = me
        if k & 1:
            other = flip(other, 1)
        if k & 2:
            other = flip(other, 2)
        return other

    barrier = pltpu.get_barrier_semaphore()
    for k in range(1, tok_count):
        pl.semaphore_signal(barrier, inc=1, device_id={"tok": tok_peer(k)}, device_id_type=MESH)
    for other in (partner, sibling):
        pl.semaphore_signal(barrier, inc=1, device_id={"task": other}, device_id_type=MESH)

    padded[...] = jnp.zeros_like(padded)
    count_rows[...] = jnp.zeros_like(count_rows)
    for read in reads:
        read.wait()
    padded[0:tokens, 0:blocks, :] = act_ref[...]
    counts = counts_ref[...]
    for owner in range(tok_count):
        mine = jnp.where(me == owner, counts, 0)
        at = pl.ds(owner * blocks_per, blocks_per)
        count_rows[0, at, :] = (mine // 16).astype(jnp.float32)
        count_rows[1, at, :] = (mine % 16).astype(jnp.float32)
    padded[tokens:tokens + 2] = count_rows[...].astype(jnp.bfloat16)
    flat = padded[...].reshape(rows * held, width)
    lane = lax.broadcasted_iota(jnp.int32, (rows, rows * held), 1)
    row = lax.broadcasted_iota(jnp.int32, (rows, rows * held), 0)
    offset = lane - held * row

    def pick(owner):
        for slot in range(slots):
            if slot < pairs:
                block = cand_ref[slot % cand_count, owner * blocks_per + slot // cand_count]
            else:
                block = owner * blocks_per + (slot - pairs)
            select[slot] = jnp.where(offset == block, 1.0, 0.0).astype(jnp.bfloat16)
        picked = jnp.dot(
            select[...].reshape(slots * rows, rows * held), flat, preferred_element_type=jnp.float32
        )
        return picked.astype(jnp.bfloat16).reshape(slots, rows, width)

    chunks = [(lo, min(lo + CHUNK, pairs)) for lo in range(0, pairs, CHUNK)] + [(pairs, slots)]
    passed = range(len(chunks) - 1)

    def z_copy(k, c, source=None):
        lo, hi = chunks[c]
        return pltpu.make_async_remote_copy(
            src_ref=sending.at[k, lo:hi], dst_ref=out_ref.at[task, me if source is None else source, lo:hi],
            send_sem=z_send.at[k, c], recv_sem=z_recv.at[k, c],
            device_id={"tok": tok_peer(k)}, device_id_type=MESH)

    def task_copy(quarter, k, c, target, send, recv):
        lo, hi = chunks[c]
        view = out_ref.at[quarter, tok_peer(k), lo:hi]
        return pltpu.make_async_remote_copy(
            src_ref=view, dst_ref=view, send_sem=send.at[k, c],
            recv_sem=recv.at[k, c], device_id={"task": target}, device_id_type=MESH)

    def pass_on(k, c):
        task_copy(task, k, c, partner, x_send, x_recv).start()
        task_copy(task, k, c, sibling, s_send, s_recv).start()

    def relay(k, c):
        task_copy(partner, k, c, partner, x_send, x_recv).wait_recv()
        task_copy(partner, k, c, sibling, r_send, r_recv).start()

    order = [k for k in ORDER if k < tok_count]
    for k in order:
        sending[k] = pick(tok_peer(k))
    out_ref[task, me] = pick(me)
    pl.semaphore_wait(barrier, tok_count + 1)
    for own in passed:
        if own == 0:
            for k in order:
                z_copy(k, 0).start()
        pass_on(0, own)
    for c in range(1, AHEAD):
        for k in order:
            z_copy(k, c).start()

    token = token_ids(out_ref.shape[1], tokens, width)

    def finish(c):
        for k in range(tok_count):
            task_copy(sibling, k, c, sibling, s_send, s_recv).wait_recv()
            task_copy(flip(sibling, 2), k, c, sibling, r_send, r_recv).wait_recv()

        def one(slot, carry):
            for quarter in range(out_ref.shape[0]):
                cols_ref[slot, :, quarter * width:(quarter + 1) * width] = standardise(
                    out_ref[quarter, :, slot], tokens, token)
            return carry

        lax.fori_loop(chunks[c][0], chunks[c][1], one, 0)

    last = len(chunks) - 1
    waiting = [(0, c) for c in passed]
    for c in passed:
        for k in order:
            z_copy(k, c, tok_peer(k)).wait_recv()
            if c + AHEAD <= last:
                z_copy(k, c + AHEAD).start()
            pass_on(k, c)
            waiting.append((k, c))
            relay(*waiting.pop(0))
        if c >= LAG:
            for at in [at for at in waiting if at[1] <= c - LAG]:
                relay(*at)
                waiting.remove(at)
            finish(c - LAG)
    for k in order:
        z_copy(k, last, tok_peer(k)).wait_recv()
    for k, c in waiting:
        relay(k, c)

    def one_row(slot, carry):
        rows = standardise(out_ref[task, :, pairs + slot], tokens, token)
        rows_ref[slot] = rows.astype(jnp.float32).T.astype(jnp.bfloat16)
        return carry

    lax.fori_loop(0, blocks_per, one_row, 0)
    for c in range(max(len(passed) - LAG, 0), len(passed)):
        finish(c)
    for k in range(tok_count):
        if k:
            for c in range(len(chunks)):
                z_copy(k, c).wait_send()
        for c in passed:
            task_copy(task, k, c, partner, x_send, x_recv).wait_send()
            task_copy(task, k, c, sibling, s_send, s_recv).wait_send()
            task_copy(partner, k, c, sibling, r_send, r_recv).wait_send()


def token_ids(sources, tokens, width):
    row = lax.broadcasted_iota(jnp.int32, (sources, ROWS, width), 1)
    source = lax.broadcasted_iota(jnp.int32, (sources, ROWS, width), 0)
    return jnp.where(row < tokens, row + source * tokens, sources * ROWS).astype(jnp.float32)


def standardise(tiles, tokens, token):
    sources, rows, width = tiles.shape
    values = tiles.astype(jnp.float32)
    count_f = jnp.sum(values[:, tokens:tokens + 1] * 16.0 + values[:, tokens + 1:tokens + 2], axis=0)
    live = token < count_f[None]
    kept = jnp.where(live, values, 0.0)
    mean = jnp.sum(jnp.sum(kept, axis=0), axis=0, keepdims=True) / count_f
    centered = jnp.where(live, values - mean[None], 0.0)
    variance = jnp.sum(jnp.sum(centered * centered, axis=0), axis=0, keepdims=True) / count_f
    scaled = centered * (lax.rsqrt(variance + 1e-05) * lax.rsqrt(count_f))[None]
    return scaled.astype(jnp.bfloat16).reshape(sources * rows, width)


def tile_kernel(cols_ref, rows_ref, out_ref, held, sems):
    step = pl.program_id(0)
    blocks_per, cand_count = held.shape[0], held.shape[1]
    left = rows_ref[step]
    for cand in range(cand_count):
        tile = jnp.dot(left, cols_ref[cand_count * step + cand], preferred_element_type=jnp.float32)
        held[step, cand] = tile.astype(jnp.bfloat16)
        pltpu.make_async_copy(held.at[step, cand], out_ref.at[step, cand], sems.at[step, cand]).start()

    @pl.when(step == blocks_per - 1)
    def _():
        for block in range(blocks_per):
            for cand in range(cand_count):
                pltpu.make_async_copy(held.at[block, cand], out_ref.at[block, cand], sems.at[block, cand]).wait()


def kernel_body(activations, counts, candidates):
    tok_count = lax.axis_size("tok")
    task_count = lax.axis_size("task")
    tokens, blocks, width = activations.shape
    blocks_per = counts.shape[0]
    cand_count = candidates.shape[1]
    pairs = blocks_per * cand_count
    slots = pairs + blocks_per
    held = (blocks + 15) // 16 * 16
    tile = (slots, ROWS, width)
    columns, rows = pl.pallas_call(
        functools.partial(exchange_kernel, tok_count, blocks_per, cand_count),
        out_shape=(
            jax.ShapeDtypeStruct((pairs, tok_count * ROWS, task_count * width), jnp.bfloat16),
            jax.ShapeDtypeStruct((blocks_per, width, tok_count * ROWS), jnp.bfloat16),
        ),
        in_specs=[
            pl.BlockSpec(memory_space=pltpu.HBM),
            pl.BlockSpec(memory_space=pltpu.HBM),
            pl.BlockSpec(memory_space=pltpu.HBM),
        ],
        out_specs=(pl.BlockSpec(memory_space=pltpu.VMEM),) * 2,
        scratch_shapes=[
            pltpu.VMEM((task_count, tok_count) + tile, jnp.bfloat16),
            pltpu.VMEM(activations.shape, jnp.bfloat16),
            pltpu.VMEM(counts.shape, jnp.int32),
            pltpu.SMEM(candidates.shape[::-1], jnp.int32),
            pltpu.SemaphoreType.DMA((3,)),
            pltpu.VMEM((ROWS, held, width), jnp.bfloat16),
            pltpu.VMEM((2, held, width), jnp.float32),
            pltpu.VMEM((slots, ROWS, ROWS * held), jnp.bfloat16),
            pltpu.VMEM((tok_count,) + tile, jnp.bfloat16),
        ] + [pltpu.SemaphoreType.DMA((tok_count, pairs // CHUNK + 2))] * 8,
        compiler_params=pltpu.CompilerParams(
            collective_id=0, has_side_effects=True, vmem_limit_bytes=32 * 2**20
        ),
        name="exchange",
    )(*[pltpu.with_memory_space_constraint(x, pltpu.HBM) for x in (activations, counts, candidates.T)])
    return pl.pallas_call(
        tile_kernel,
        grid=(blocks_per,),
        out_shape=jax.ShapeDtypeStruct((blocks_per, cand_count, width, width * task_count), jnp.bfloat16),
        in_specs=[pl.BlockSpec(memory_space=pltpu.VMEM)] * 2,
        out_specs=pl.BlockSpec(memory_space=pltpu.HBM),
        scratch_shapes=[
            pltpu.VMEM((blocks_per, cand_count, width, width * task_count), jnp.bfloat16),
            pltpu.SemaphoreType.DMA((blocks_per, cand_count)),
        ],
        compiler_params=pltpu.CompilerParams(vmem_limit_bytes=32 * 2**20),
        name="tiles",
    )(columns, rows)


def solution(mesh):
    small = mesh.shape["tok"] == 4 and mesh.shape["task"] == 4
    return jax.shard_map(
        kernel_body if small else body,
        mesh=mesh,
        in_specs=(P("tok", "layer", "task"), P(("layer", "tok"), "task"), P("layer", None)),
        out_specs=P("tok", "layer", "task", None),
        check_vma=False,
    )
```
